1024 devices in a mesh: gx: 32 (over z_hi, y, core), gy: 32 (over z_lo, x).
Axes of the slice: x: 4, y: 4, z: 32 (z_hi: 4, z_lo: 8; z = z_hi * 8 + z_lo), core: 2. Of those that a mesh axis runs over, the one named last changes fastest.
Arguments:
- position: float32 [32, 32, 3, 4096], P('gx', 'gy'), may hold values from 0 to 32, as said below
- velocity: float32 [32, 32, 3, 4096], P('gx', 'gy'), may hold values from -6 to 6
- mass: float32 [32, 32, 1, 4096], P('gx', 'gy'), may hold values from 0.3 to 3
- pair_list: int32 [32, 32, 32, 27], P('gx', 'gy'), may hold values from 0 to 287, as said below
- hot_leaf: int32 [32, 32, 8], P('gx', 'gy'), may hold values from 0 to 32, as said below
Outputs:
- displacement: float32 [32, 32, 3, 4096], P('gx', 'gy')
- new_velocity: float32 [32, 32, 3, 4096], P('gx', 'gy')
The draws below stay inside these ranges and needn't reach their ends.
Inputs may be any that keep to these rules, and one draw needn't show every extreme that they name: `pair_list`: entry k of every list names a leaf of neighbourhood block k mod 9. `position`: component 0 of a particle of cell (i, j) lies in [i, i + 1), component 1 in [j, j + 1), component 2 in [0, 1). `hot_leaf`: the slots of a cell hold distinct leaf numbers first and the empty mark 32 after them; cell (i, j) and cell (i, (j + 16) mod 32) hold exactly 8 hot leaves together.
All inputs are finite; a program needn't handle non-finite values.
Results may differ from the reference program's by a relative error of at most 0.00023.
Values sent between devices are 32-bit elements; how exact they have to be, the bound alone decides.
No kernel may reach another device: no remote copies, remote signals or barrier semaphores. Data moves between devices by JAX's collectives and lax.ppermute only.
A program may use at most 32 MiB of HBM per device.

```python
import math
import jax
import jax.numpy as jnp
from jax import lax

LEAF = 128
LEAF_DEV = 32
PAIRS = 27
HOT = 8
PART = 4096
NGX = 32
NGY = 32
N_GX = 32
N_GY = 32


def draw_position(key, part):
    shape = (N_GX, N_GY, 3, LEAF_DEV * LEAF)
    inside = jax.random.uniform(key, shape, jnp.float32)
    row_index = lax.broadcasted_iota(jnp.int32, shape, 0).astype(jnp.float32)
    column_index = lax.broadcasted_iota(jnp.int32, shape, 1).astype(jnp.float32)
    channel = lax.broadcasted_iota(jnp.int32, shape, 2)
    offset = jnp.where(channel == 0, row_index, 0.0) + jnp.where(channel == 1, column_index, 0.0)
    return inside + offset


def draw_pair_list(key, part):
    shape = (N_GX, N_GY, LEAF_DEV, PAIRS)
    chosen = jax.random.randint(key, shape, 0, LEAF_DEV, jnp.int32)
    block = lax.broadcasted_iota(jnp.int32, shape, 3) % 9
    return block * LEAF_DEV + chosen


def draw_hot_leaf(key, part):
    first_key = jax.random.fold_in(key, 11)
    second_key = jax.random.fold_in(key, 23)
    half = N_GY // 2
    lower = jax.random.randint(first_key, (N_GX, half), 0, HOT + 1, jnp.int32)
    counts = jnp.concatenate([lower, HOT - lower], axis=1)
    scores = jax.random.randint(second_key, (N_GX, N_GY, LEAF_DEV), 0, 1 << 20, jnp.int32)
    leaves = lax.broadcasted_iota(jnp.int32, (N_GX, N_GY, LEAF_DEV), 2)
    order = jnp.argsort(scores * LEAF_DEV + leaves, axis=-1).astype(jnp.int32)[:, :, :HOT]
    slots = lax.broadcasted_iota(jnp.int32, (N_GX, N_GY, HOT), 2)
    return jnp.where(slots < counts[:, :, None], order, LEAF_DEV).astype(jnp.int32)


def shard_levels(stream_key, dims, cuts, low, top_value):
    def one(dim, shards_of):
        draws = jax.random.uniform(jax.random.fold_in(jax.random.fold_in(stream_key, 6), dim), (shards_of,), jnp.float32, low / len(cuts), top_value / len(cuts))
        return jnp.repeat(jnp.exp(draws), dims[dim] // shards_of).reshape((-1,) + (1,) * (len(dims) - dim - 1))

    level = one(*cuts[0])
    for cut in cuts[1:]:
        level = level * one(*cut)
    return level


def normal_values(rng, shape, scale, limit, shards=(), kind=jnp.bfloat16):
    array = scale * jax.random.normal(rng, shape, jnp.float32)
    if shards:
        array = array * shard_levels(rng, shape, shards, -0.22, 0.18)
    return jnp.clip(array, -limit, limit).astype(kind)


def setup_inputs(seed: int = 0) -> dict:
    keys = jax.random.split(jax.random.key(seed), 6)
    return {
        "position": draw_position(jax.random.fold_in(keys[5], 71), 0),
        "velocity": normal_values(keys[1], (NGX, NGY, 3, PART), 1.0, 6.0, ((0, 32), (1, 32)), jnp.float32),
        "mass": jnp.clip(jnp.exp(math.log(3.0) - 2.3025851 * jax.random.uniform(keys[2], (NGX, NGY, 1, PART), jnp.float32) ** shard_levels(keys[2], (NGX, NGY, 1, PART), ((0, 32), (1, 32)), -0.2, 0.2)), 0.3, 3.0),
        "pair_list": draw_pair_list(jax.random.fold_in(keys[5], 71), 0),
        "hot_leaf": draw_hot_leaf(jax.random.fold_in(keys[5], 71), 0),
    }


kernel_scale = 1.0
viscosity = 0.5
time_step = 0.5
base_entries = 9


def source_leaves(extended):
    channels = extended.shape[2]
    count = extended.shape[3] // LEAF
    return jnp.transpose(extended, (2, 0, 1, 3)).reshape(channels, 9 * count, LEAF)


def own_leaves(own):
    channels = own.shape[0]
    count = own.shape[1] // LEAF
    return jnp.transpose(own.reshape(channels, count, LEAF), (1, 0, 2))


def inverse_density(own, extended, pairs, usage):
    sources = source_leaves(extended)

    def one_leaf(inputs):
        target, chosen, used = inputs
        picked = jnp.take(sources, chosen, axis=1)
        near_mass = (picked[6] * used[:, None]).reshape(-1)
        near = picked.reshape(sources.shape[0], -1)
        diff = target[0:3, :, None] - near[0:3, None, :]
        weight = jnp.exp(-jnp.sum(diff * diff, axis=0) / kernel_scale)
        rho = target[6] + jnp.sum(near_mass[None, :] * weight, axis=1)
        return 1.0 / rho

    result = lax.map(one_leaf, (own_leaves(own), pairs, usage))
    return result.reshape(1, -1)


def acceleration(own, own_inverse, extended, extended_inverse, pairs, usage):
    sources = source_leaves(extended)
    source_inverse = source_leaves(extended_inverse)[0]
    targets = own_leaves(own)
    target_inverse = own_inverse.reshape(-1, LEAF)

    def one_leaf(inputs):
        target, target_q, chosen, used = inputs
        picked = jnp.take(sources, chosen, axis=1)
        near_mass = (picked[6] * used[:, None]).reshape(-1)
        near = picked.reshape(sources.shape[0], -1)
        near_q = jnp.take(source_inverse, chosen, axis=0).reshape(-1)
        diff = target[0:3, :, None] - near[0:3, None, :]
        weight = jnp.exp(-jnp.sum(diff * diff, axis=0) / kernel_scale)
        massed = near_mass[None, :] * weight
        press = massed * (2.0 / kernel_scale) * (target_q[:, None] + near_q[None, :])
        pushed = jnp.sum(press[None] * diff, axis=2)
        damped = jnp.sum((massed * near_q[None, :])[None] * (near[3:6, None, :] - target[3:6, :, None]), axis=2)
        return pushed + viscosity * damped

    result = lax.map(one_leaf, (targets, target_inverse, pairs, usage))
    return jnp.transpose(result, (1, 0, 2)).reshape(3, -1)


def neighbourhood(field):
    rows, columns = field.shape[0], field.shape[1]
    padded = jnp.pad(field, ((1, 1), (1, 1), (0, 0), (0, 0)))
    blocks = jnp.stack([jnp.stack([padded[a:a + rows, b:b + columns] for b in range(3)], axis=2) for a in range(3)], axis=2)
    return blocks.reshape((rows * columns, 3, 3) + field.shape[2:])


def entry_usage(flat_hot):
    leaves = jnp.arange(LEAF_DEV, dtype=jnp.int32)
    is_hot = jnp.any(flat_hot[:, :, None] == leaves[None, None, :], axis=1)
    entries = jnp.arange(PAIRS, dtype=jnp.int32)
    used = (entries[None, None, :] < base_entries) | is_hot[:, :, None]
    return jnp.where(used, 1.0, 0.0).astype(jnp.float32)


def section_all(position, velocity, mass, pair_list, hot_leaf):
    rows, columns = position.shape[0], position.shape[1]
    own = jnp.concatenate([position, velocity, mass], axis=2)
    flat_own = own.reshape((rows * columns,) + own.shape[2:])
    flat_pairs = pair_list.reshape((rows * columns,) + pair_list.shape[2:])
    usage = entry_usage(hot_leaf.reshape(rows * columns, -1))
    extended = neighbourhood(own)
    inverse = lax.map(lambda z: inverse_density(z[0], z[1], z[2], z[3]), (flat_own, extended, flat_pairs, usage))
    extended_inverse = neighbourhood(inverse.reshape(rows, columns, 1, -1))
    acc = lax.map(lambda z: acceleration(z[0], z[1], z[2], z[3], z[4], z[5]), (flat_own, inverse, extended, extended_inverse, flat_pairs, usage))
    return acc.reshape(position.shape)


def reference(position, velocity, mass, pair_list, hot_leaf):
    first = section_all(position, velocity, mass, pair_list, hot_leaf)
    mid_position = position + 0.5 * time_step * velocity
    mid_velocity = velocity + 0.5 * time_step * first
    second = section_all(mid_position, mid_velocity, mass, pair_list, hot_leaf)
    return time_step * mid_velocity, velocity + time_step * second
```

```python
import functools
import math
import jax
import jax.numpy as jnp
from jax import lax
from jax.experimental import pallas as pl
from jax.experimental.pallas import tpu as pltpu
from jax.sharding import PartitionSpec as P

LEAF = 128
CELLS = 9
BASE = 9
time_step = 0.5
F32 = jnp.float32
BF16 = jnp.bfloat16
ROOT = math.sqrt(math.log2(math.e))
VM = 56 * 2**20


def halves(a):
    hi = a.astype(BF16)
    return hi, (a - hi.astype(F32)).astype(BF16)


def thirds(a):
    hi = a.astype(BF16).astype(F32)
    rest = a - hi
    mid = rest.astype(BF16).astype(F32)
    return hi, mid, rest - mid


def columns_of(e_ref, origin_ref, cell, start, width, drift):
    r = e_ref[cell, :, pl.ds(start, width)]
    x = r[0:3] - origin_ref[0:3, 0:1]
    v = r[3:6]
    if drift:
        x = x + drift * v
    return x, v, r[6:7]


def prepare_sources(e_ref, origin_ref, s_ref, drift, slot, width=1024):
    leaves = e_ref.shape[2] // LEAF
    per = width // LEAF

    def step(i, _):
        cell = i // (leaves // per)
        part = i % (leaves // per)
        x, _, m = columns_of(e_ref, origin_ref, cell, pl.multiple_of(part * width, width), width, drift)
        y = x * ROOT
        c = jnp.where(m > 0, jnp.log2(m), -1000.0) - jnp.sum(y * y, axis=0, keepdims=True)
        h, d, l = thirds(jnp.concatenate([2.0 * y, c, jnp.ones_like(c), jnp.zeros_like(y)], axis=0))
        g = jnp.concatenate([h, d, h, l], axis=0).astype(BF16)
        for k in range(per):
            s_ref[(slot + cell) * leaves + part * per + k] = g[:, k * LEAF:(k + 1) * LEAF]
        return 0

    lax.fori_loop(0, e_ref.shape[0] * leaves // per, step, 0)


def target_rows(e_ref, origin_ref, drift):
    width = e_ref.shape[2]
    x, _, _ = columns_of(e_ref, origin_ref, 0, 0, width, drift)
    y = x * ROOT
    n = -jnp.sum(y * y, axis=0, keepdims=True)
    h, d, l = thirds(jnp.concatenate([y, jnp.ones_like(n), n, jnp.zeros_like(y)], axis=0))
    z = jnp.zeros_like(h)
    return jnp.concatenate([h, h, d, d, l, h, z, z], axis=0).astype(BF16)


def source_rows(s_ref, leaf):
    s = s_ref[leaf]
    return jnp.concatenate([s[0:16], s[0:16], s[16:32], s[16:32]], axis=0)


def weights(s_ref, t, chosen):
    s = jnp.concatenate([source_rows(s_ref, leaf)[0:48] for leaf in chosen], axis=1)
    return jnp.exp2(jnp.dot(t, s, preferred_element_type=F32))


def against(a, b):
    return lax.dot_general(a, b, (((1,), (1,)), ((), ())), preferred_element_type=F32)


def groups(begin, end, size=2):
    return [range(k, min(k + size, end)) for k in range(begin, end, size)]


def every_leaf(hot_ref, leaves, entries, group, together, part, store, add):
    def base(i, _):
        for g in range(group):
            store(i * group + g, part(i * group + g, 0, BASE))
        return 0

    lax.fori_loop(0, leaves // group, base, 0)
    for begin in range(0, hot_ref.shape[0], together):
        @pl.when(hot_ref[begin] < leaves)
        def _():
            for slot in range(begin, begin + together):
                leaf = jnp.minimum(hot_ref[slot], leaves - 1)
                alive = jnp.where(hot_ref[slot] < leaves, 1.0, 0.0)
                add(leaf, alive * part(leaf, BASE, entries))


def density_kernel(drift, group, together, pair_ref, hot_ref, e_ref, e1_ref, e2_ref, origin_ref, q_ref, s_ref, t_ref, sum_ref):
    leaves = e_ref.shape[2] // LEAF
    for i, ref in enumerate((e_ref, e1_ref, e2_ref)):
        prepare_sources(ref, origin_ref, s_ref, drift, 3 * i)
    rows = target_rows(e_ref, origin_ref, drift)
    for leaf in range(leaves):
        t = rows[:, leaf * LEAF:(leaf + 1) * LEAF]
        t_ref[leaf] = jnp.concatenate([t, t], axis=0).T

    def part(leaf, begin, end):
        t = t_ref[leaf][:, 0:48]
        total = jnp.zeros((LEAF, LEAF), F32)
        for ks in groups(begin, end):
            w = weights(s_ref, t, [pair_ref[leaf, k] for k in ks])
            for i in range(len(ks)):
                total = total + w[:, i * LEAF:(i + 1) * LEAF]
        return total

    def store(leaf, value):
        sum_ref[leaf] = value

    def add(leaf, value):
        sum_ref[leaf] = sum_ref[leaf] + value

    every_leaf(hot_ref, leaves, pair_ref.shape[1], group, together, part, store, add)
    ones = jnp.ones((8, 3 * LEAF), BF16)
    for leaf in range(leaves):
        at = slice(leaf * LEAF, (leaf + 1) * LEAF)
        total = jnp.concatenate([a.astype(BF16) for a in thirds(sum_ref[leaf])], axis=1)
        q_ref[0:1, at] = 1.0 / (e_ref[0, 6:7, at] + against(ones, total)[0:1])


def density(drift, pairs, hot, extended, origin, group=16, together=4):
    part = extended[0].shape[2]
    leaves = part // LEAF
    return pl.pallas_call(
        functools.partial(density_kernel, drift, group, together),
        out_shape=(
            jax.ShapeDtypeStruct((1, part), F32),
            jax.ShapeDtypeStruct((CELLS * leaves, 32, LEAF), BF16),
        ),
        in_specs=[pl.BlockSpec(memory_space=pltpu.SMEM)] * 2 + [pl.BlockSpec(memory_space=pltpu.VMEM)] * 4,
        out_specs=[pl.BlockSpec(memory_space=pltpu.VMEM)] * 2,
        scratch_shapes=[pltpu.VMEM((leaves, LEAF, LEAF), BF16), pltpu.VMEM((leaves, LEAF, LEAF), F32)],
        compiler_params=pltpu.CompilerParams(vmem_limit_bytes=VM),
        name="density",
    )(pairs, hot, *extended, origin)


def prepare_moments(e_ref, v_ref, origin_ref, g_ref, drift, slot, width=1024):
    leaves = e_ref.shape[2] // LEAF
    per = width // LEAF

    def step(i, _):
        cell = i // (leaves // per)
        part = i % (leaves // per)
        start = pl.multiple_of(part * width, width)
        x, v, _ = columns_of(e_ref, origin_ref, cell, start, width, drift)
        if drift:
            v = v_ref[cell, 0:3, pl.ds(start, width)]
            q = v_ref[cell, 3:4, pl.ds(start, width)]
        else:
            q = v_ref[cell, :, pl.ds(start, width)]
        z = jnp.zeros_like(q)
        g = jnp.concatenate([q * x, q, z, x, q * v, z, z, z, z, z], axis=0)
        both = jnp.concatenate(halves(g), axis=0)
        for k in range(per):
            g_ref[(slot + cell) * leaves + part * per + k] = both[:, k * LEAF:(k + 1) * LEAF]
        return 0

    lax.fori_loop(0, e_ref.shape[0] * leaves // per, step, 0)


def accel_kernel(drift, group, together, pair_ref, hot_ref, e_ref, e1_ref, e2_ref, v_ref, v1_ref, v2_ref, s_ref, origin_ref, acc_ref, t_ref, g_ref, sum_ref):
    leaves = e_ref.shape[2] // LEAF
    for i, refs in enumerate(((e_ref, v_ref), (e1_ref, v1_ref), (e2_ref, v2_ref))):
        prepare_moments(*refs, origin_ref, g_ref, drift, 3 * i)

    t_ref[...] = target_rows(e_ref, origin_ref, drift)

    def part(leaf, begin, end):
        t = t_ref[:, pl.ds(pl.multiple_of(leaf * LEAF, LEAF), LEAF)]
        z = jnp.zeros_like(t)
        two = jnp.concatenate([jnp.concatenate([t, z], axis=1), jnp.concatenate([z, t], axis=1)], axis=0)
        total = jnp.zeros((32, 2 * LEAF), F32)
        for ks in groups(begin, end):
            n = len(ks)
            chosen = [pair_ref[leaf, k] for k in ks]
            s = jnp.concatenate([source_rows(s_ref, c) for c in (chosen + chosen)[0:2]], axis=0).T
            hi, lo = halves(jnp.exp2(jnp.dot(s, two if n == 2 else two[:, :LEAF], preferred_element_type=F32)))
            at = [slice(i * LEAF, (i + 1) * LEAF) for i in range(n)]
            r = jnp.concatenate([jnp.concatenate([hi[:, a], lo[:, a]], axis=1) for a in at], axis=0)
            g = jnp.concatenate([g_ref[c] for c in chosen], axis=1)
            total = total + jnp.dot(g, r, preferred_element_type=F32)
        return total[0:16, :LEAF] + (total[0:16, LEAF:] + (total[16:32, :LEAF] + total[16:32, LEAF:]))

    def store(leaf, value):
        sum_ref[leaf] = value

    def add(leaf, value):
        sum_ref[leaf] = sum_ref[leaf] + value

    every_leaf(hot_ref, leaves, pair_ref.shape[1], group, together, part, store, add)
    for leaf in range(leaves):
        at = slice(leaf * LEAF, (leaf + 1) * LEAF)
        x, v, m = columns_of(e_ref, origin_ref, 0, leaf * LEAF, LEAF, drift)
        if drift:
            v, q = v_ref[0, 0:3, at], v_ref[0, 3:4, at]
        else:
            q = v_ref[0, :, at]
        s0 = 1.0 / q - m
        o = sum_ref[leaf]
        s3, s2, s1, s4 = o[0:3], o[3:4], o[5:8], o[8:11]
        acc_ref[:, at] = 2.0 * (q * (x * s0 - s1) + (x * s2 - s3)) + 0.5 * (s4 - v * s2)


def accel(drift, pairs, hot, extended, fresh, kept, origin, group=16, together=4):
    part = extended[0].shape[2]
    leaves = part // LEAF
    return pl.pallas_call(
        functools.partial(accel_kernel, drift, group, together),
        out_shape=jax.ShapeDtypeStruct((3, part), F32),
        in_specs=[pl.BlockSpec(memory_space=pltpu.SMEM)] * 2 + [pl.BlockSpec(memory_space=pltpu.VMEM)] * 8,
        out_specs=pl.BlockSpec(memory_space=pltpu.VMEM),
        scratch_shapes=[
            pltpu.VMEM((64, part), BF16),
            pltpu.VMEM((CELLS * leaves, 32, LEAF), BF16),
            pltpu.VMEM((leaves, 16, LEAF), F32),
        ],
        compiler_params=pltpu.CompilerParams(vmem_limit_bytes=VM),
        name="accel",
    )(pairs, hot, *extended, *fresh, *kept, origin)


def swaps(cells, axis):
    count = lax.axis_size(axis)
    got = []
    for first in (0, 1):
        pairs = [(i, i + 1) for i in range(first, count - 1, 2)]
        got.append(lax.ppermute(cells, axis, pairs + [(b, a) for a, b in pairs]))
    return got


def surround(own):
    here = jnp.stack([own] + swaps(own, "gx"))
    return [here] + swaps(here, "gy")


def slot_of(block_step, axis):
    even = lax.axis_index(axis) % 2 == 0
    return jnp.where(block_step == 1, 0, jnp.where((block_step == 2) == even, 1, 2))


def to_slots(pairs, leaves):
    block = pairs // leaves
    return (3 * slot_of(block % 3, "gy") + slot_of(block // 3, "gx")) * leaves + pairs % leaves


def cell_origin():
    row = lax.axis_index("gx").astype(F32) + 0.5
    column = lax.axis_index("gy").astype(F32) + 0.5
    middle = jnp.stack([row, column, jnp.full_like(row, 0.5)] + [jnp.zeros_like(row)] * 5)
    return jnp.broadcast_to(middle[:, None], (8, LEAF))


def local(position, velocity, mass, pair_list, hot_leaf):
    pairs = to_slots(pair_list[0, 0], pair_list.shape[2])
    hot = hot_leaf[0, 0]
    half = 0.5 * time_step
    origin = cell_origin()
    speed = velocity[0, 0]
    extended = surround(jnp.concatenate([position[0, 0], speed, mass[0, 0]], axis=0))
    first_inverse, *first_kept = density(0.0, pairs, hot, extended, origin)
    second_inverse, *second_kept = density(half, pairs, hot, extended, origin)
    first = accel(0.0, pairs, hot, extended, surround(first_inverse), first_kept, origin)
    mid_speed = speed + half * first
    later = surround(jnp.concatenate([mid_speed, second_inverse], axis=0))
    second = accel(half, pairs, hot, extended, later, second_kept, origin)
    return ((time_step * mid_speed)[None, None], (speed + time_step * second)[None, None])


def solution(mesh):
    return jax.shard_map(
        local,
        mesh=mesh,
        in_specs=(
            P("gx", "gy", None, None),
            P("gx", "gy", None, None),
            P("gx", "gy", None, None),
            P("gx", "gy", None, None),
            P("gx", "gy", None),
        ),
        out_specs=(P("gx", "gy", None, None), P("gx", "gy", None, None)),
        check_vma=False,
    )
```

```python
import functools
import math
import jax
import jax.numpy as jnp
from jax import lax
from jax.experimental import pallas as pl
from jax.experimental.pallas import tpu as pltpu
from jax.sharding import PartitionSpec as P

LEAF = 128
CELLS = 9
BASE = 9
time_step = 0.5
viscosity = 0.5
F32 = jnp.float32
BF16 = jnp.bfloat16
ROOT = math.sqrt(math.log2(math.e))
VM = 24 * 2**20


def halves(a):
    hi = a.astype(BF16)
    return hi, (a - hi.astype(F32)).astype(BF16)


def thirds(a):
    hi = a.astype(BF16).astype(F32)
    rest = a - hi
    mid = rest.astype(BF16).astype(F32)
    return hi, mid, rest - mid


def row_index(width):
    return lax.broadcasted_iota(jnp.int32, (8, width), 0)


def eight(a):
    return jnp.concatenate([a, jnp.zeros((8 - a.shape[0], a.shape[1]), a.dtype)], axis=0)


def centred(state, origin_ref, drift):
    r = eight(state)
    row = row_index(r.shape[1])
    x = r - jnp.where(row == 0, origin_ref[0], jnp.where(row == 1, origin_ref[1], 0.5))
    if drift:
        x = x + drift * pltpu.roll(r, 5, 0)
    return jnp.where(row < 3, x, r)


def squared(x, row):
    y = x * ROOT
    return y, jnp.sum(jnp.where(row < 3, y * y, 0.0), axis=0, keepdims=True)


def prepare_sources(e_ref, origin_ref, s_ref, drift, slot, width=1024):
    leaves = e_ref.shape[2] // LEAF
    per = width // LEAF
    row = row_index(width)

    def step(i, _):
        cell = i // (leaves // per)
        part = i % (leaves // per)
        r = centred(e_ref[cell, :, pl.ds(pl.multiple_of(part * width, width), width)], origin_ref, drift)
        y, size = squared(r, row)
        c = jnp.where(r > 0, jnp.log2(r), -1000.0) - size
        h, d, l = thirds(jnp.where(row < 3, 2.0 * y, jnp.where(row == 3, 1.0, jnp.where(row == 6, c, 0.0))))
        g = jnp.concatenate([h, d, h, l], axis=0).astype(BF16)
        for k in range(per):
            s_ref[(slot + cell) * leaves + part * per + k] = g[:, k * LEAF:(k + 1) * LEAF]
        return 0

    lax.fori_loop(0, e_ref.shape[0] * leaves // per, step, 0)


def target_rows(e_ref, origin_ref, drift):
    r = centred(e_ref[0], origin_ref, drift)
    row = row_index(r.shape[1])
    y, size = squared(r, row)
    h, d, l = thirds(jnp.where(row < 3, y, jnp.where(row == 3, -size, jnp.where(row == 6, 1.0, 0.0))))
    z = jnp.zeros_like(h)
    return jnp.concatenate([h, h, d, d, l, h, z, z], axis=0).astype(BF16)


def source_rows(s_ref, leaf):
    s = s_ref[leaf]
    return jnp.concatenate([s[0:16], s[0:16], s[16:32], s[16:32]], axis=0)


def weights(s_ref, t, chosen):
    s = jnp.concatenate([source_rows(s_ref, leaf)[0:48] for leaf in chosen], axis=1)
    return jnp.exp2(jnp.dot(t, s, preferred_element_type=F32))


def against(a, b):
    return lax.dot_general(a, b, (((1,), (1,)), ((), ())), preferred_element_type=F32)


def groups(begin, end, size=2):
    return [range(k, min(k + size, end)) for k in range(begin, end, size)]


def every_leaf(hot_ref, leaves, entries, group, together, part, store, add):
    def base(i, _):
        for g in range(group):
            store(i * group + g, part(i * group + g, 0, BASE))
        return 0

    lax.fori_loop(0, leaves // group, base, 0)
    for begin in range(0, hot_ref.shape[0], together):
        @pl.when(hot_ref[begin] < leaves)
        def _():
            for slot in range(begin, begin + together):
                leaf = jnp.minimum(hot_ref[slot], leaves - 1)
                alive = jnp.where(hot_ref[slot] < leaves, 1.0, 0.0)
                add(leaf, alive * part(leaf, BASE, entries))


def density_kernel(drift, group, together, pair_ref, hot_ref, origin_ref, e_ref, e1_ref, e2_ref, q_ref, s_ref, t_ref, sum_ref):
    leaves = e_ref.shape[2] // LEAF
    for i, ref in enumerate((e_ref, e1_ref, e2_ref)):
        prepare_sources(ref, origin_ref, s_ref, drift, 3 * i)
    rows = target_rows(e_ref, origin_ref, drift)
    for leaf in range(leaves):
        t = rows[:, leaf * LEAF:(leaf + 1) * LEAF]
        t_ref[leaf] = jnp.concatenate([t, t], axis=0).T

    def part(leaf, begin, end):
        t = t_ref[leaf][:, 0:48]
        total = jnp.zeros((LEAF, LEAF), F32)
        for ks in groups(begin, end):
            w = weights(s_ref, t, [pair_ref[leaf, k] for k in ks])
            for i in range(len(ks)):
                total = total + w[:, i * LEAF:(i + 1) * LEAF]
        return total

    def store(leaf, value):
        sum_ref[leaf] = value

    def add(leaf, value):
        sum_ref[leaf] = sum_ref[leaf] + value

    every_leaf(hot_ref, leaves, pair_ref.shape[1], group, together, part, store, add)
    ones = jnp.ones((8, 3 * LEAF), BF16)
    for leaf in range(leaves):
        at = slice(leaf * LEAF, (leaf + 1) * LEAF)
        total = jnp.concatenate([a.astype(BF16) for a in thirds(sum_ref[leaf])], axis=1)
        q_ref[0:1, at] = 1.0 / (e_ref[0, 6:7, at] + against(ones, total)[0:1])


def density(drift, pairs, hot, origin, extended, group=32, together=8):
    part = extended[0].shape[2]
    leaves = part // LEAF
    return pl.pallas_call(
        functools.partial(density_kernel, drift, group, together),
        out_shape=(
            jax.ShapeDtypeStruct((1, part), F32),
            jax.ShapeDtypeStruct((CELLS * leaves, 32, LEAF), BF16),
        ),
        in_specs=[pl.BlockSpec(memory_space=pltpu.SMEM)] * 3 + [pl.BlockSpec(memory_space=pltpu.VMEM)] * 3,
        out_specs=[pl.BlockSpec(memory_space=pltpu.VMEM)] * 2,
        scratch_shapes=[pltpu.VMEM((leaves, LEAF, LEAF), BF16), pltpu.VMEM((leaves, LEAF, LEAF), F32)],
        compiler_params=pltpu.CompilerParams(vmem_limit_bytes=VM),
        name="density",
    )(pairs, hot, origin, *extended)


def prepare_moments(e_ref, v_ref, origin_ref, g_ref, drift, slot, width=1024):
    leaves = e_ref.shape[2] // LEAF
    per = width // LEAF
    row = row_index(width)

    def step(i, _):
        cell = i // (leaves // per)
        part = i % (leaves // per)
        at = pl.ds(pl.multiple_of(part * width, width), width)
        r = centred(e_ref[cell, :, at], origin_ref, drift)
        if drift:
            fresh = v_ref[cell, :, at]
            q = fresh[3:4]
            r = jnp.where(row < 3, r, pltpu.roll(eight(fresh), 3, 0))
        else:
            q = v_ref[cell, :, at]
        r = jnp.where(row < 6, r, 1.0)
        both = jnp.concatenate(halves(jnp.concatenate([q * r, r], axis=0)), axis=0)
        for k in range(per):
            g_ref[(slot + cell) * leaves + part * per + k] = both[:, k * LEAF:(k + 1) * LEAF]
        return 0

    lax.fori_loop(0, e_ref.shape[0] * leaves // per, step, 0)


def accel_kernel(drift, group, together, pair_ref, hot_ref, origin_ref, e_ref, e1_ref, e2_ref, v_ref, v1_ref, v2_ref, s_ref, *rest):
    if drift:
        out_ref, t_ref, g_ref, sum_ref = rest
    else:
        next_ref, out_ref, mid_ref, t_ref, g_ref, sum_ref = rest
    leaves = e_ref.shape[2] // LEAF
    for i, refs in enumerate(((e_ref, v_ref), (e1_ref, v1_ref), (e2_ref, v2_ref))):
        prepare_moments(*refs, origin_ref, g_ref, drift, 3 * i)
    t_ref[...] = target_rows(e_ref, origin_ref, drift)

    def part(leaf, begin, end):
        t = t_ref[:, pl.ds(pl.multiple_of(leaf * LEAF, LEAF), LEAF)]
        z = jnp.zeros_like(t)
        two = jnp.concatenate([jnp.concatenate([t, z], axis=1), jnp.concatenate([z, t], axis=1)], axis=0)
        total = jnp.zeros((32, 2 * LEAF), F32)
        for ks in groups(begin, end):
            n = len(ks)
            chosen = [pair_ref[leaf, k] for k in ks]
            s = jnp.concatenate([source_rows(s_ref, c) for c in (chosen + chosen)[0:2]], axis=0).T
            hi, lo = halves(jnp.exp2(jnp.dot(s, two if n == 2 else two[:, :LEAF], preferred_element_type=F32)))
            at = [slice(i * LEAF, (i + 1) * LEAF) for i in range(n)]
            r = jnp.concatenate([jnp.concatenate([hi[:, a], lo[:, a]], axis=1) for a in at], axis=0)
            g = jnp.concatenate([g_ref[c] for c in chosen], axis=1)
            total = total + jnp.dot(g, r, preferred_element_type=F32)
        return total[0:16, :LEAF] + (total[0:16, LEAF:] + (total[16:32, :LEAF] + total[16:32, LEAF:]))

    def store(leaf, value):
        sum_ref[leaf] = value

    def add(leaf, value):
        sum_ref[leaf] = sum_ref[leaf] + value

    every_leaf(hot_ref, leaves, pair_ref.shape[1], group, together, part, store, add)
    half = 0.5 * time_step
    for leaf in range(leaves):
        at = slice(leaf * LEAF, (leaf + 1) * LEAF)
        r = centred(e_ref[0, :, at], origin_ref, drift)
        x, m, speed = r[0:3], r[6:7], r[3:6]
        if drift:
            v, q = v_ref[0, 0:3, at], v_ref[0, 3:4, at]
        else:
            v, q = speed, v_ref[0, :, at]
        o = sum_ref[leaf]
        s3, s4, s2, s1 = o[0:3], o[3:6], o[6:7], o[8:11]
        acc = 2.0 * (q * (x * (1.0 / q - m) - s1) + (x * s2 - s3)) + viscosity * (s4 - v * s2)
        if drift:
            out = speed + time_step * acc
        else:
            mid = speed + half * acc
            mid_ref[0:3, at] = mid
            mid_ref[3:4, at] = next_ref[0:1, at]
            out = time_step * mid
        for i in range(3):
            out_ref[i, 0:1, at] = out[i:i + 1]


def accel(drift, pairs, hot, origin, extended, fresh, kept, following=None, group=32, together=8):
    part = extended[0].shape[2]
    leaves = part // LEAF
    out = jax.ShapeDtypeStruct((3, 1, part), F32)
    more = [] if drift else [following]
    return pl.pallas_call(
        functools.partial(accel_kernel, drift, group, together),
        out_shape=out if drift else (out, jax.ShapeDtypeStruct((4, part), F32)),
        in_specs=[pl.BlockSpec(memory_space=pltpu.SMEM)] * 3 + [pl.BlockSpec(memory_space=pltpu.VMEM)] * (7 + len(more)),
        out_specs=pl.BlockSpec(memory_space=pltpu.VMEM) if drift else [pl.BlockSpec(memory_space=pltpu.VMEM)] * 2,
        scratch_shapes=[
            pltpu.VMEM((64, part), BF16),
            pltpu.VMEM((CELLS * leaves, 32, LEAF), BF16),
            pltpu.VMEM((leaves, 16, LEAF), F32),
        ],
        compiler_params=pltpu.CompilerParams(vmem_limit_bytes=VM),
        name="accel",
    )(pairs, hot, origin, *extended, *fresh, kept, *more)


def swaps(cells, axis):
    count = lax.axis_size(axis)
    got = []
    for first in (0, 1):
        pairs = [(i, i + 1) for i in range(first, count - 1, 2)]
        got.append(lax.ppermute(cells, axis, pairs + [(b, a) for a, b in pairs]))
    return got


def surround(own):
    here = jnp.stack([own] + swaps(own, "gx"))
    return [here] + swaps(here, "gy")


def slot_of(block_step, axis):
    even = lax.axis_index(axis) % 2 == 0
    return jnp.where(block_step == 1, 0, jnp.where((block_step == 2) == even, 1, 2))


def to_slots(pairs, leaves):
    block = pairs // leaves
    return (3 * slot_of(block % 3, "gy") + slot_of(block // 3, "gx")) * leaves + pairs % leaves


def local(position, velocity, mass, pair_list, hot_leaf):
    pairs = to_slots(pair_list[0, 0], pair_list.shape[2])
    hot = hot_leaf[0, 0]
    half = 0.5 * time_step
    origin = jnp.stack([lax.axis_index("gx"), lax.axis_index("gy")]).astype(F32) + 0.5
    extended = surround(jnp.concatenate([position[0, 0], velocity[0, 0], mass[0, 0]], axis=0))
    inverse, kept = density(0.0, pairs, hot, origin, extended)
    traded = swaps(inverse, "gx")
    later_inverse, later_kept = density(half, pairs, hot, origin, extended)
    *traded, later_inverse = lax.optimization_barrier((*traded, later_inverse))
    here = jnp.stack([inverse] + traded)
    inverses = [here] + swaps(here, "gy")
    displacement, mid = accel(0.0, pairs, hot, origin, extended, inverses, kept, later_inverse)
    new_velocity = accel(half, pairs, hot, origin, extended, surround(mid), later_kept)
    return displacement.reshape(velocity.shape), new_velocity.reshape(velocity.shape)


def solution(mesh):
    return jax.shard_map(
        local,
        mesh=mesh,
        in_specs=(
            P("gx", "gy", None, None),
            P("gx", "gy", None, None),
            P("gx", "gy", None, None),
            P("gx", "gy", None, None),
            P("gx", "gy", None),
        ),
        out_specs=(P("gx", "gy", None, None), P("gx", "gy", None, None)),
        check_vma=False,
    )
```
